512 devices in a mesh: sib: 2 (over core), row: 16 (over z, y_lo), col: 16 (over x, y_hi).
Axes of the slice: x: 4, y: 8 (y_hi: 4, y_lo: 2; y = y_hi * 2 + y_lo), z: 8, core: 2. Of those that a mesh axis runs over, the one named last changes fastest.
Arguments:
- child_front: float32 [2, 8192, 8192], P('sib', 'row', 'col'), may hold values from -6 to 6
- child_panel: float32 [2, 8192, 1024], P('sib', ('row', 'col')), may hold values from -0.42 to 0.42
- block_map: int32 [2, 64], replicated, may hold values from 0 to 95, as said below
- parent_front: float32 [12288, 12288], P(('row', 'sib'), 'col'), may hold values from -6 to 6
- pivot_inverse: float32 [512, 512], replicated, may hold values from -0.03 to 0.1, as said below
Outputs:
- parent_out: float32 [12288, 12288], P(('row', 'sib'), 'col')
The draws below stay inside these ranges and needn't reach their ends.
Inputs may be any that keep to these rules, and one draw needn't show every extreme that they name: `block_map`: each row is strictly increasing. A child block i that lands in parent block g * 6 + k with 0 <= k < 6 satisfies g * 4 - 2 <= i < (g + 1) * 4; the lower end is met for g = 1 in every draw, and the last parent block is always named. `pivot_inverse`: lower triangular with diagonal entries from 0.05 to 0.1.
All inputs are finite; a program needn't handle non-finite values.
Results may differ from the reference program's by a relative error of at most 0.0001.
Values sent between devices are 32-bit elements; how exact they have to be, the bound alone decides.
A program may use at most 64 MiB of HBM per device.

```python
import jax
import jax.numpy as jnp
from jax import lax

BLK = 128
CBD = 4
PIV = 4
KC = 1024
PBD = 6
HB = 2
NCB = 64
CHILD = 8192
PARENT = 12288
PANEL = 512


def sibling_map(key, groups):
    key_steps, key_slots = jax.random.split(key)
    group_index = jnp.arange(groups + 1, dtype=jnp.int32)
    raw_steps = jax.random.randint(key_steps, (groups + 1,), -HB, 1, dtype=jnp.int32)
    offsets = jnp.where((group_index == 0) | (group_index == groups), 0, jnp.where(group_index == 1, PBD - PIV - CBD, raw_steps))
    counts = CBD + offsets[1:] - offsets[:-1]
    slot_index = jnp.arange(PBD, dtype=jnp.int32)
    scores = jax.random.randint(key_slots, (groups, PBD), 0, 1 << 20, dtype=jnp.int32) * PBD + slot_index[None, :]
    row_group = jnp.arange(groups, dtype=jnp.int32)[:, None]
    forced = (row_group == groups - 1) & (slot_index[None, :] == PBD - 1)
    scores = jnp.where(forced, -1, scores)
    slot_ranks = jnp.argsort(jnp.argsort(scores, axis=1), axis=1)
    chosen_flat = (slot_ranks < counts[:, None]).reshape(-1)
    position = jnp.arange(groups * PBD, dtype=jnp.int32)
    sorted_slots = jnp.argsort(jnp.where(chosen_flat, position, position + groups * PBD))
    return sorted_slots[:NCB].astype(jnp.int32)


def draw_block_map(key, part):
    groups = NCB // CBD
    first_map = sibling_map(jax.random.fold_in(key, 11), groups)
    second_map = sibling_map(jax.random.fold_in(key, 12), groups)
    return jnp.stack([first_map, second_map])


def draw_pivot_inverse(key, part):
    key_diag, key_low = jax.random.split(jax.random.fold_in(key, 29))
    row_index = jnp.arange(PANEL)[:, None]
    col_index = jnp.arange(PANEL)[None, :]
    lower = 0.005 * jax.random.truncated_normal(key_low, -4.0, 4.0, (PANEL, PANEL), jnp.float32)
    diagonal = jax.random.uniform(key_diag, (PANEL,), jnp.float32, 0.05, 0.1)
    return jnp.where(row_index > col_index, lower, 0.0) + jnp.where(row_index == col_index, diagonal[:, None], 0.0)


def steps_of(key, extent, cuts, low, high):
    def one(dim, parts):
        draws = jax.random.uniform(jax.random.fold_in(jax.random.fold_in(key, 6), dim), (parts,), jnp.float32, low / len(cuts), high / len(cuts))
        return jnp.repeat(jnp.exp(draws), extent[dim] // parts).reshape((-1,) + (1,) * (len(extent) - dim - 1))

    gain = one(*cuts[0])
    for cut in cuts[1:]:
        gain = gain * one(*cut)
    return gain


def scatter_about(key, dims, scale, limit, shards=(), kind=jnp.bfloat16):
    drawn = scale * jax.random.normal(key, dims, jnp.float32)
    if shards:
        drawn = drawn * steps_of(key, dims, shards, -0.22, 0.18)
    return jnp.clip(drawn, -limit, limit).astype(kind)


def setup_inputs(seed: int = 0) -> dict:
    arg_keys = jax.random.split(jax.random.key(seed), 6)
    return {
        "child_front": scatter_about(arg_keys[0], (2, CHILD, CHILD), 1.0, 6.0, ((0, 2), (1, 16), (2, 16)), jnp.float32),
        "child_panel": scatter_about(arg_keys[1], (2, CHILD, KC), 0.07, 0.42, ((0, 2), (1, 256)), jnp.float32),
        "block_map": draw_block_map(jax.random.fold_in(arg_keys[5], 71), 0),
        "parent_front": scatter_about(arg_keys[3], (PARENT, PARENT), 1.0, 6.0, ((0, 32), (1, 16)), jnp.float32),
        "pivot_inverse": draw_pivot_inverse(jax.random.fold_in(arg_keys[5], 71), 0),
    }


def schur_child(front_block, panel_block):
    return front_block - jnp.dot(panel_block, panel_block.T, precision=lax.Precision.HIGHEST, preferred_element_type=jnp.float32)


def reference(child_front, child_panel, block_map, parent_front, pivot_inverse):
    child_order = child_front.shape[1]
    parent_order = parent_front.shape[0]
    child_blocks = child_order // BLK
    parent_blocks = parent_order // BLK
    assembled = parent_front.reshape(parent_blocks, BLK, parent_blocks, BLK).transpose(0, 2, 1, 3)
    for sibling in range(2):
        update = schur_child(child_front[sibling], child_panel[sibling])
        update_tiles = update.reshape(child_blocks, BLK, child_blocks, BLK).transpose(0, 2, 1, 3)
        rows_map = block_map[sibling].astype(jnp.int32)
        assembled = assembled.at[rows_map[:, None], rows_map[None, :]].add(update_tiles)
    assembled = assembled.transpose(0, 2, 1, 3).reshape(parent_order, parent_order)
    factor_rows = jnp.dot(assembled[:, :PANEL], pivot_inverse.T, precision=lax.Precision.HIGHEST, preferred_element_type=jnp.float32)
    lower_rows = factor_rows[PANEL:]
    trailing = assembled[PANEL:, PANEL:] - jnp.dot(lower_rows, lower_rows.T, precision=lax.Precision.HIGHEST, preferred_element_type=jnp.float32)
    result = assembled.at[PANEL:, PANEL:].set(trailing)
    return result.at[:, :PANEL].set(factor_rows)
```

```python
import functools

import jax
import jax.numpy as jnp
from jax import lax
from jax.experimental import pallas as pl
from jax.experimental.pallas import tpu as pltpu
from jax.sharding import PartitionSpec as P

BLK = 128
CBD = 4
PBD = 6
HB = 2
PANEL = 512
MESH = pl.DeviceIdType.MESH
F32 = jnp.float32
BF16 = jnp.bfloat16


def halves(value):
    high = value.astype(BF16)
    return high, (value - high.astype(F32)).astype(BF16)


def dot_nt(a, b):
    return lax.dot_general(a, b, (((1,), (1,)), ((), ())), preferred_element_type=F32)


def product_nt(a, b):
    a_high, a_low = a
    b_high, b_low = b
    return dot_nt(a_high, b_high) + (dot_nt(a_high, b_low) + dot_nt(a_low, b_high))


class Links:
    def __init__(self, send_sems, recv_sems):
        self.send_sems, self.recv_sems = send_sems, recv_sems
        self.used = 0
        self.sent = []

    def new(self):
        self.used += 1
        return self.used - 1

    def copy(self, k, src, dst, device):
        return pltpu.make_async_remote_copy(
            src_ref=src,
            dst_ref=dst,
            send_sem=self.send_sems.at[k],
            recv_sem=self.recv_sems.at[k],
            device_id=device,
            device_id_type=MESH,
        )

    def send(self, k, src, dst, device):
        made = self.copy(k, src, dst, device)
        made.start()
        self.sent.append(made)

    def arrived(self, k, ref, device):
        self.copy(k, ref, ref, device).wait_recv()

    def drain(self):
        for made in self.sent:
            made.wait_send()
        self.sent = []


def gather_both(links, place, own, rows_buf, cols_buf, cut):
    s, r, c = place
    z, yl = r // 2, lax.rem(r, 2)
    x, yh = c // 4, lax.rem(c, 4)
    depth = rows_buf.shape[1]
    top, low = pl.ds(0, cut), pl.ds(cut, depth - cut)

    def cy(dx, dy):
        return lax.rem(x + dx + 4, 4) * 4 + lax.rem(yh + dy + 4, 4)

    def rz(dz, flip=0):
        side = 1 - yl if flip else yl
        return lax.rem(z + dz + 8, 8) * 2 + side

    def at_col(j):
        return (s, r, j)

    def at_row(i):
        return (s, i, c)

    yp, ym = at_col(cy(0, 1)), at_col(cy(0, -1))
    xp, xm = at_col(cy(1, 0)), at_col(cy(-1, 0))
    zp, zm = at_row(rz(1)), at_row(rz(-1))
    pair = at_row(rz(0, 1))

    events = []

    def when(t, fn):
        events.append((t, len(events), fn))

    k_yp, k_ym = links.new(), links.new()
    links.send(k_yp, own, rows_buf.at[c], yp)
    links.send(k_ym, own, rows_buf.at[c], ym)
    k_t = links.new()
    transposed = (s, c, r)

    @pl.when(r != c)
    def _():
        links.copy(k_t, own, cols_buf.at[c], transposed).start()

    @pl.when(r == c)
    def _():
        pltpu.make_async_copy(own, cols_buf.at[r], links.recv_sems.at[k_t]).start()

    k_x = {}
    for name in ("own", "-1", "+1", "2"):
        k_x[name] = (links.new(), links.new(), links.new(), links.new())

    def spread_x(name, dy, src=None):
        kp, km, _, _ = k_x[name]
        slot = cy(0, dy)
        src = rows_buf.at[slot] if src is None else src
        links.send(kp, src, rows_buf.at[slot], xp)
        links.send(km, src, rows_buf.at[slot], xm)

    spread_x("own", 0, own)
    k_y2p, k_y2m = links.new(), links.new()

    def from_ym():
        slot = cy(0, -1)
        links.arrived(k_yp, rows_buf.at[slot], ym)
        links.send(k_y2p, rows_buf.at[slot, top], rows_buf.at[slot, top], yp)
        spread_x("-1", -1)

    def from_yp():
        slot = cy(0, 1)
        links.arrived(k_ym, rows_buf.at[slot], yp)
        links.send(k_y2m, rows_buf.at[slot, low], rows_buf.at[slot, low], ym)
        spread_x("+1", 1)

    def far_y():
        slot = cy(0, 2)
        links.arrived(k_y2p, rows_buf.at[slot, top], ym)
        links.arrived(k_y2m, rows_buf.at[slot, low], yp)
        spread_x("2", 2)

    def relay_x(name, dy):
        kp, km, k2p, k2m = k_x[name]
        slot_m, slot_p = cy(-1, dy), cy(1, dy)
        links.arrived(kp, rows_buf.at[slot_m], xm)
        links.send(k2p, rows_buf.at[slot_m, top], rows_buf.at[slot_m, top], xp)
        links.arrived(km, rows_buf.at[slot_p], xp)
        links.send(k2m, rows_buf.at[slot_p, low], rows_buf.at[slot_p, low], xm)

    def far_x(name, dy):
        _, _, k2p, k2m = k_x[name]
        slot = cy(2, dy)
        links.arrived(k2p, rows_buf.at[slot, top], xm)
        links.arrived(k2m, rows_buf.at[slot, low], xp)

    when(5, from_ym)
    when(5, from_yp)
    when(4, lambda: relay_x("own", 0))
    when(10, far_y)
    when(10, lambda: relay_x("-1", -1))
    when(11, lambda: relay_x("+1", 1))
    when(16, lambda: relay_x("2", 2))
    when(90, lambda: [far_x(n, d) for n, d in (("own", 0), ("-1", -1), ("+1", 1), ("2", 2))])

    k_pair = links.new()
    k_z = {(f, d): (links.new(), links.new()) for f in (0, 1) for d in (1, 2, 3, 4)}

    def step_z(flip, d):
        kp, km = k_z[flip, d]
        up, down = cols_buf.at[rz(1 - d, flip)], cols_buf.at[rz(d - 1, flip)]
        if d == 4:
            up, down = up.at[top], down.at[low]
        links.send(kp, up, up, zp)
        links.send(km, down, down, zm)

    def arrive_z(flip, d):
        kp, km = k_z[flip, d]
        from_m, from_p = cols_buf.at[rz(-d, flip)], cols_buf.at[rz(d, flip)]
        if d == 4:
            from_m, from_p = from_m.at[top], from_p.at[low]
        links.arrived(kp, from_m, zm)
        links.arrived(km, from_p, zp)

    def from_transposed():
        links.arrived(k_t, cols_buf.at[r], transposed)
        links.send(k_pair, cols_buf.at[r], cols_buf.at[r], pair)
        step_z(0, 1)

    def from_pair():
        slot = rz(0, 1)
        links.arrived(k_pair, cols_buf.at[slot], pair)
        step_z(1, 1)

    def relay_z(flip, d):
        arrive_z(flip, d)
        if d < 4:
            step_z(flip, d + 1)

    when(7, from_transposed)
    when(9, from_pair)
    for d in (1, 2, 3, 4):
        when(7 + 5 * d, lambda d=d: relay_z(0, d))
        when(9 + 5 * d, lambda d=d: relay_z(1, d))

    for _, _, fn in sorted(events, key=lambda e: e[:2]):
        fn()

    @pl.when(r != c)
    def _():
        links.copy(k_t, own, cols_buf.at[c], transposed).wait_send()


def picks(block_map, child, group):
    weights = {}
    for w in range(CBD + HB):
        i = lax.rem(group * CBD - HB + w + 64, 64)
        mark = block_map[child, i] - group * PBD
        for q in range(max(0, w - HB), min(PBD, w + HB + 1)):
            weights[w, q] = (mark == q).astype(F32)
    return weights


def placed_sum(weights, q, block):
    total = None
    for w in range(CBD + HB):
        if (w, q) in weights:
            term = weights[w, q] * block(w)
            total = term if total is None else total + term
    return total


def kernel(
    front, panel, block_map, parent, inverse, out_ref,
    rows_buf, cols_buf, front_v, parent_v, inverse_v,
    wide, tall, leave, come, assembled, f_out, f_rows, f_cols, out_v,
    a_high, a_low, send_sems, recv_sems, local_sems,
):
    s, r, c = lax.axis_index("sib"), lax.axis_index("row"), lax.axis_index("col")
    place = (s, r, c)
    z, yl = r // 2, lax.rem(r, 2)
    x, yh = c // 4, lax.rem(c, 4)
    links = Links(send_sems, recv_sems)
    sib = (1 - s, r, c)

    loads = [
        pltpu.make_async_copy(src, dst, local_sems.at[k])
        for k, (src, dst) in enumerate(
            ((front.at[0], front_v), (parent, parent_v), (inverse, inverse_v),
             (panel.at[0], rows_buf.at[c]))
        )
    ]
    for load in loads:
        load.start()

    barrier = pltpu.get_barrier_semaphore()

    def greet(device):
        pl.semaphore_signal(barrier, inc=1, device_id=device, device_id_type=MESH)

    def col_at(dx, dy):
        return (s, r, lax.rem(x + dx + 4, 4) * 4 + lax.rem(yh + dy + 4, 4))

    for device in (col_at(0, 1), col_at(0, -1), col_at(1, 0), col_at(-1, 0)):
        greet(device)
    for dz in (1, -1):
        greet((s, lax.rem(z + dz + 8, 8) * 2 + yl, c))
    greet((s, z * 2 + 1 - yl, c))
    greet(sib)
    pl.when(r != c)(lambda: greet((s, c, r)))
    pl.when(c > 0)(lambda: greet((s, r, c - 1)))
    pl.when(r > 0)(lambda: greet((s, r - 1, c)))
    pl.when(c > 0)(lambda: greet((s, r, 0)))
    def one_if(test):
        return test.astype(jnp.int32)

    pl.semaphore_wait(barrier, 8 + one_if(r != c) + one_if(c < 15) + one_if(r < 15) + 15 * one_if(c == 0))

    gather_both(links, place, panel.at[0], rows_buf, cols_buf, 16)
    loads[3].wait()
    loads[0].wait()

    depth = rows_buf.shape[1] * 16
    high, low = halves(rows_buf[...].reshape(depth, rows_buf.shape[2]))
    a_high[...] = high
    a_low[...] = low
    for n in range(2):
        b = halves(cols_buf[8 * n : 8 * n + 8].reshape(depth // 2, cols_buf.shape[2]))
        prod = product_nt((a_high[...], a_low[...]), b)
        for w in range(2):
            col = n * 2 + w
            wide[HB + col] = front_v[:, col * BLK : (col + 1) * BLK] - prod[:, w * BLK : (w + 1) * BLK]

    k_col = links.new()
    tail, head = wide.at[pl.ds(CBD, HB)], wide.at[pl.ds(0, HB)]
    col_copy = links.copy(k_col, tail, head, (s, r, lax.rem(c + 1, 16)))
    pl.when(c < 15)(col_copy.start)
    pl.when(c > 0)(col_copy.wait_recv)

    edge = HB * BLK

    @pl.when(c == 0)
    def _():
        wide[0:HB] = jnp.zeros((HB,) + wide.shape[1:], F32)

    @pl.when(r == 0)
    def _():
        tall[:, 0:edge, :] = jnp.zeros((PBD, edge, BLK), F32)

    pick = picks(block_map, s, c)
    for q in range(PBD):
        tall[q, edge:, :] = placed_sum(pick, q, lambda w: wide[w])

    k_row = links.new()
    width = pl.ds(0, PBD)
    row_copy = links.copy(
        k_row, tall.at[width, pl.ds(CBD * BLK, edge)], tall.at[width, pl.ds(0, edge)],
        (s, lax.rem(r + 1, 16), c),
    )
    pl.when(r < 15)(row_copy.start)
    pl.when(r > 0)(row_copy.wait_recv)

    pick = picks(block_map, s, r)
    half = PBD // 2
    k_sib = links.new()

    def blocks(q):
        return lambda w: tall[q, w * BLK : (w + 1) * BLK, :]

    for k in range(PBD):
        for q in range(PBD):
            leave[k, q] = placed_sum(pick, k, blocks(q))
    links.send(k_sib, leave.at[pl.ds(half * (1 - s), half)], come, sib)
    loads[1].wait()
    for k in range(half):
        for q in range(PBD):
            at = (slice(k * BLK, (k + 1) * BLK), slice(q * BLK, (q + 1) * BLK))
            assembled[at] = parent_v[at] + leave[half * s + k, q]
    links.arrived(k_sib, come, sib)
    for k in range(half):
        for q in range(PBD):
            at = (slice(k * BLK, (k + 1) * BLK), slice(q * BLK, (q + 1) * BLK))
            assembled[at] += come[k, q]

    loads[2].wait()
    k_scatter = [links.new() for _ in range(16)]

    @pl.when(c == 0)
    def _():
        factor = product_nt(halves(assembled[:, :PANEL]), halves(inverse_v[...]))
        f_out[...] = factor.reshape(f_rows.shape)
        f_rows[0] = f_out[0]
        copies = [
            pltpu.make_async_remote_copy(
                src_ref=f_out.at[j], dst_ref=f_rows.at[j],
                send_sem=links.send_sems.at[k_scatter[j]], recv_sem=links.recv_sems.at[k_scatter[0]],
                device_id=(s, r, jnp.int32(j)), device_id_type=MESH)
            for j in range(1, 16)
        ]
        for made in copies:
            made.start()
        for made in copies:
            made.wait_send()

    @pl.when(c > 0)
    def _():
        links.arrived(k_scatter[0], f_rows.at[c], (s, r, 0))

    gather_both(links, place, f_rows.at[c], f_rows, f_cols.at[s], 8)
    k_swap = links.new()
    links.send(k_swap, f_cols.at[s], f_cols.at[s], sib)
    links.arrived(k_swap, f_cols.at[1 - s], sib)

    f_all = f_rows[...].reshape(assembled.shape[0], PANEL)
    g_all = f_cols[...].reshape(assembled.shape[1], PANEL)
    fh = halves(f_all)
    parent_rows, parent_cols = assembled.shape
    for n in range(3):
        span = slice(n * 256, (n + 1) * 256)
        prod = product_nt(fh, halves(g_all[span]))
        row_at = (r * 2 + s) * parent_rows + lax.broadcasted_iota(jnp.int32, prod.shape, 0)
        col_at_ = c * parent_cols + n * 256 + lax.broadcasted_iota(jnp.int32, prod.shape, 1)
        inside = (row_at >= PANEL) & (col_at_ >= PANEL)
        now = assembled[:, span]
        done = jnp.where(inside, now - prod, now)
        if n < 2:
            done = jnp.where(c == 0, f_all[:, span], done)
        out_v[:, span] = done
    store = pltpu.make_async_copy(out_v, out_ref, local_sems.at[0])
    store.start()

    links.drain()
    pl.when(c < 15)(col_copy.wait_send)
    pl.when(r < 15)(row_copy.wait_send)
    store.wait()
    assert links.used <= 144, links.used


def shards(front, panel, block_map, parent, inverse):
    anywhere = pl.BlockSpec(memory_space=pl.ANY)
    rows, cols = parent.shape
    kc = panel.shape[2]
    return pl.pallas_call(
        kernel,
        out_shape=jax.ShapeDtypeStruct(parent.shape, F32),
        in_specs=[anywhere, anywhere, pl.BlockSpec(memory_space=pltpu.SMEM), anywhere, anywhere],
        out_specs=anywhere,
        scratch_shapes=[
            pltpu.VMEM((16, 32, kc), F32),
            pltpu.VMEM((16, 32, kc), F32),
            pltpu.VMEM((512, 512), F32),
            pltpu.VMEM((rows, cols), F32),
            pltpu.VMEM((PANEL, PANEL), F32),
            pltpu.VMEM((CBD + HB, 512, BLK), F32),
            pltpu.VMEM((PBD, 768, BLK), F32),
            pltpu.VMEM((PBD, PBD, BLK, BLK), F32),
            pltpu.VMEM((3, PBD, BLK, BLK), F32),
            pltpu.VMEM((rows, cols), F32),
            pltpu.VMEM((16, 24, PANEL), F32),
            pltpu.VMEM((16, 24, PANEL), F32),
            pltpu.VMEM((2, 16, 24, PANEL), F32),
            pltpu.VMEM((rows, cols), F32),
            pltpu.VMEM((512, kc), BF16),
            pltpu.VMEM((512, kc), BF16),
            pltpu.SemaphoreType.DMA((144,)),
            pltpu.SemaphoreType.DMA((144,)),
            pltpu.SemaphoreType.DMA((4,)),
        ],
        compiler_params=pltpu.CompilerParams(
            collective_id=0, has_side_effects=True, vmem_limit_bytes=50 * 2**20
        ),
        name="front_step",
    )(front, panel, block_map, parent, inverse)


def solution(mesh):
    placed = (
        P("sib", "row", "col"), P("sib", ("row", "col"), None), P(),
        P(("row", "sib"), "col"), P(),
    )
    return jax.shard_map(
        shards, mesh=mesh, in_specs=placed, out_specs=P(("row", "sib"), "col"), check_vma=False
    )
```

```python
import functools

import jax
import jax.numpy as jnp
from jax import lax
from jax.experimental import pallas as pl
from jax.experimental.pallas import tpu as pltpu
from jax.sharding import PartitionSpec as P

BLK = 128
CBD = 4
PBD = 6
HB = 2
PANEL = 512
MESH = pl.DeviceIdType.MESH
F32 = jnp.float32
BF16 = jnp.bfloat16


def halves(value):
    high = value.astype(BF16)
    return high, (value - high.astype(F32)).astype(BF16)


def dot_nt(a, b):
    return lax.dot_general(a, b, (((1,), (1,)), ((), ())), preferred_element_type=F32)


def product_nt(a, b):
    a_high, a_low = a
    b_high, b_low = b
    return dot_nt(a_high, b_high) + (dot_nt(a_high, b_low) + dot_nt(a_low, b_high))


class Links:
    def __init__(self, send_sems, recv_sems):
        self.send_sems, self.recv_sems = send_sems, recv_sems
        self.used = 0
        self.sent = []

    def new(self):
        self.used += 1
        return self.used - 1

    def copy(self, k, src, dst, device, k_recv=None):
        return pltpu.make_async_remote_copy(
            src_ref=src,
            dst_ref=dst,
            send_sem=self.send_sems.at[k],
            recv_sem=self.recv_sems.at[k if k_recv is None else k_recv],
            device_id=device,
            device_id_type=MESH,
        )

    def send(self, k, src, dst, device):
        made = self.copy(k, src, dst, device)
        made.start()
        self.sent.append(made)

    def arrived(self, k, ref, device):
        self.copy(k, ref, ref, device).wait_recv()

    def drain(self):
        for made in self.sent:
            made.wait_send()
        self.sent = []


class Ring:
    def __init__(self, links, place):
        self.links = links
        self.s, self.r, self.c = s, r, c = place
        self.z, self.yl = r // 2, lax.rem(r, 2)
        self.x, self.yh = c // 4, lax.rem(c, 4)
        self.yp, self.ym = self.at_col(self.cy(0, 1)), self.at_col(self.cy(0, -1))
        self.xp, self.xm = self.at_col(self.cy(1, 0)), self.at_col(self.cy(-1, 0))
        self.zp, self.zm = self.at_row(self.rz(1)), self.at_row(self.rz(-1))
        self.pair = self.at_row(self.rz(0, 1))
        self.sib = (1 - s, r, c)
        self.events = []

    def cy(self, dx, dy):
        return lax.rem(self.x + dx + 4, 4) * 4 + lax.rem(self.yh + dy + 4, 4)

    def rz(self, dz, flip=0):
        side = 1 - self.yl if flip else self.yl
        return lax.rem(self.z + dz + 8, 8) * 2 + side

    def at_col(self, j):
        return (self.s, self.r, j)

    def at_row(self, i):
        return (self.s, i, self.c)

    def when(self, t, fn):
        self.events.append((t, len(self.events), fn))

    def run(self, until=1e9):
        ready = sorted((e for e in self.events if e[0] < until), key=lambda e: e[:2])
        self.events = [e for e in self.events if e[0] >= until]
        for _, _, fn in ready:
            fn()


def gather_rows(ring, own, rows_buf, cut, times):
    links, c = ring.links, ring.c
    cy, yp, ym, xp, xm = ring.cy, ring.yp, ring.ym, ring.xp, ring.xm
    depth = rows_buf.shape[1]
    top, low = pl.ds(0, cut), pl.ds(cut, depth - cut)
    k_yp, k_ym = links.new(), links.new()
    links.send(k_yp, own, rows_buf.at[c], yp)
    links.send(k_ym, own, rows_buf.at[c], ym)
    k_x = {}
    for dy in (0, -1, 1, 2):
        k_x[dy] = (links.new(), links.new(), links.new(), links.new())

    def spread_x(dy, src=None):
        kp, km, _, _ = k_x[dy]
        slot = cy(0, dy)
        src = rows_buf.at[slot] if src is None else src
        links.send(kp, src, rows_buf.at[slot], xp)
        links.send(km, src, rows_buf.at[slot], xm)

    spread_x(0, own)
    k_y2p, k_y2m = links.new(), links.new()

    def from_ym():
        slot = cy(0, -1)
        links.arrived(k_yp, rows_buf.at[slot], ym)
        links.send(k_y2p, rows_buf.at[slot, top], rows_buf.at[slot, top], yp)
        spread_x(-1)

    def from_yp():
        slot = cy(0, 1)
        links.arrived(k_ym, rows_buf.at[slot], yp)
        links.send(k_y2m, rows_buf.at[slot, low], rows_buf.at[slot, low], ym)
        spread_x(1)

    def far_y():
        slot = cy(0, 2)
        links.arrived(k_y2p, rows_buf.at[slot, top], ym)
        links.arrived(k_y2m, rows_buf.at[slot, low], yp)
        spread_x(2)

    def relay_x(dy):
        kp, km, k2p, k2m = k_x[dy]
        slot_m, slot_p = cy(-1, dy), cy(1, dy)
        links.arrived(kp, rows_buf.at[slot_m], xm)
        links.send(k2p, rows_buf.at[slot_m, top], rows_buf.at[slot_m, top], xp)
        links.arrived(km, rows_buf.at[slot_p], xp)
        links.send(k2m, rows_buf.at[slot_p, low], rows_buf.at[slot_p, low], xm)

    def far_x(dy):
        _, _, k2p, k2m = k_x[dy]
        slot = cy(2, dy)
        links.arrived(k2p, rows_buf.at[slot, top], xm)
        links.arrived(k2m, rows_buf.at[slot, low], xp)

    ring.when(times[0], from_ym)
    ring.when(times[0], from_yp)
    ring.when(times[1], lambda: relay_x(0))
    ring.when(times[2], far_y)
    ring.when(times[3], lambda: relay_x(-1))
    ring.when(times[4], lambda: relay_x(1))
    ring.when(times[5], lambda: relay_x(2))
    ring.when(times[6], lambda: [far_x(dy) for dy in (0, -1, 1, 2)])


def gather_cols_ring(ring, first, cols_buf, t, gap, end):
    links = ring.links
    rz, pair, zp, zm = ring.rz, ring.pair, ring.zp, ring.zm
    depth = cols_buf.shape[1]
    cut = depth // 16 * 8
    parts = (pl.ds(0, cut), pl.ds(cut, depth - cut))
    k_pair = links.new()
    k_z = {(flip, d): (links.new(), links.new()) for flip in (0, 1) for d in (1, 2, 3, 4)}

    def piece(dz, flip, d, way):
        ref = cols_buf.at[rz(dz, flip)]
        return ref.at[parts[way < 0]] if d == 4 else ref

    def step(flip, d):
        for way, k in zip((1, -1), k_z[flip, d]):
            ref = piece(way * (1 - d), flip, d, way)
            links.send(k, ref, ref, zp if way > 0 else zm)

    def relay(flip, d):
        for way, k in zip((1, -1), k_z[flip, d]):
            links.arrived(k, piece(-way * d, flip, d, way), zm if way > 0 else zp)
            if d < 4:
                ref = piece(-way * d, flip, d + 1, way)
                links.send(k_z[flip, d + 1][way < 0], ref, ref, zp if way > 0 else zm)

    def from_first():
        first()
        ref = cols_buf.at[rz(0)]
        links.send(k_pair, ref, ref, pair)
        step(0, 1)

    def from_pair():
        links.arrived(k_pair, cols_buf.at[rz(0, 1)], pair)
        step(1, 1)

    ring.when(t, from_first)
    ring.when(t + gap / 2, from_pair)
    for d in (1, 2, 3, 4):
        ring.when(end if d == 4 else t + gap * d, lambda d=d: relay(0, d))
        ring.when(end if d == 4 else t + gap * (d + 0.5), lambda d=d: relay(1, d))


def gather_cols_two(ring, first, cols_buf, come_buf, times):
    links, yl = ring.links, ring.yl
    rz, pair, sib = ring.rz, ring.pair, ring.sib
    depth = cols_buf.shape[1]
    cut = depth // 16 * 8
    parts = {1: pl.ds(0, cut), -1: pl.ds(cut, depth - cut)}
    k_pair = links.new()
    k_z = {(flip, d): links.new() for flip in (0, 1) for d in (1, -1, 2, -2, 3, -3, 4, -4)}
    k_sib = {(flip, d): links.new() for flip in (0, 1) for d in range(-3, 5)}

    def piece(flip, d):
        ref = cols_buf.at[rz(-d, flip)]
        return ref.at[parts[1 if d > 0 else -1]] if abs(d) == 4 else ref

    def arrived(flip, d):
        links.arrived(k_z[flip, d], piece(flip, d), ring.at_row(rz(-d, flip if abs(d) < 3 else 0)))

    def to_sib(flip, d):
        links.send(k_sib[flip, d], cols_buf.at[rz(d, flip)], cols_buf.at[rz(d, flip)], sib)

    def from_first():
        first()
        ref = cols_buf.at[rz(0)]
        for d in (2, -2, 1, -1):
            for flip in (1, 0):
                links.send(k_z[flip, d], ref, ref, ring.at_row(rz(d, flip)))
        links.send(k_pair, ref, ref, pair)
        to_sib(0, 0)

    def from_near(d):
        for flip in (0, 1):
            arrived(flip, d)
            if abs(d) == 2:
                for e in (3, 4):
                    way = 1 if d > 0 else -1
                    ref = cols_buf.at[rz(-d, flip)]
                    ref = ref.at[parts[way]] if e == 4 else ref
                    links.send(k_z[flip, way * e], ref, ref, ring.at_row(rz(way * (e - 2))))
            to_sib(flip, -d)

    def from_pair():
        links.arrived(k_pair, cols_buf.at[rz(0, 1)], pair)
        to_sib(1, 0)

    def from_far():
        for flip in (0, 1):
            for d in (3, -3):
                arrived(flip, d)
                to_sib(flip, -d)
        for flip in (0, 1):
            arrived(flip, 4)
            arrived(flip, -4)
            to_sib(flip, 4)

    def from_sib():
        for (flip, d), k in k_sib.items():
            links.arrived(k, come_buf.at[rz(d, flip)], sib)

    ring.when(times[0], from_first)
    for d in (2, -2):
        ring.when(times[1], lambda d=d: from_near(d))
    ring.when(times[2], from_pair)
    for d in (1, -1):
        ring.when(times[2], lambda d=d: from_near(d))
    ring.when(times[3], from_far)
    ring.when(times[4], from_sib)


def transpose_whole(ring, own, cols_buf):
    links, s, r, c = ring.links, ring.s, ring.r, ring.c
    k = links.new()
    there = (s, c, r)

    @pl.when(r != c)
    def _():
        links.copy(k, own, cols_buf.at[c], there).start()

    @pl.when(r == c)
    def _():
        pltpu.make_async_copy(own, cols_buf.at[r], links.recv_sems.at[k]).start()

    def sent():
        @pl.when(r != c)
        def _():
            links.copy(k, own, cols_buf.at[c], there).wait_send()

    return (lambda: links.arrived(k, cols_buf.at[r], there)), sent


def transpose_parts(ring, own, cols_buf):
    links, s, r, c = ring.links, ring.s, ring.r, ring.c
    k = [links.new(), links.new()]
    k_send = [links.new(), links.new()]
    part, at = c // 8, lax.rem(c, 8)
    rows = [pl.ds(0, 16), pl.ds(16, 16)]

    def here(h):
        return (r == c) & (at * 2 + h == r)

    def copy(h, p):
        return links.copy(k_send[h], own.at[rows[h]], cols_buf.at[p, at * 2 + h], (s, at * 2 + h, r), k[p])

    for h in (0, 1):
        for p in (0, 1):

            @pl.when(jnp.logical_not(here(h)) & (part == p))
            def _():
                copy(h, p).start()

            @pl.when(here(h) & (part == p))
            def _():
                pltpu.make_async_copy(own.at[rows[h]], cols_buf.at[p, r], links.recv_sems.at[k[p]]).start()

    def sent():
        for h in (0, 1):

            @pl.when(jnp.logical_not(here(h)))
            def _():
                copy(h, 0).wait_send()

    def arrived(p):
        return lambda: links.arrived(k[p], cols_buf.at[p, r], (s, c, p * 8 + ring.z))

    return arrived, sent


def picks(block_map, child, group):
    weights = {}
    for w in range(CBD + HB):
        i = lax.rem(group * CBD - HB + w + 64, 64)
        mark = block_map[child, i] - group * PBD
        for q in range(max(0, w - HB), min(PBD, w + HB + 1)):
            weights[w, q] = (mark == q).astype(F32)
    return weights


def placed_sum(weights, q, block):
    total = None
    for w in range(CBD + HB):
        if (w, q) in weights:
            term = weights[w, q] * block(w)
            total = term if total is None else total + term
    return total


def kernel(
    front, panel, block_map, parent, inverse, out_ref,
    rows_buf, cols_buf, front_v, parent_v, inverse_v,
    wide, tall, leave, come, assembled, f_out, f_rows, f_cols, out_v,
    a_high, a_low, send_sems, recv_sems, local_sems,
):
    s, r, c = lax.axis_index("sib"), lax.axis_index("row"), lax.axis_index("col")
    place = (s, r, c)
    z, yl = r // 2, lax.rem(r, 2)
    x, yh = c // 4, lax.rem(c, 4)
    links = Links(send_sems, recv_sems)
    sib = (1 - s, r, c)

    loads = [
        pltpu.make_async_copy(src, dst, local_sems.at[k])
        for k, (src, dst) in enumerate(
            ((front.at[0], front_v), (parent, parent_v), (inverse, inverse_v),
             (panel.at[0], rows_buf.at[c]))
        )
    ]
    for load in loads:
        load.start()

    barrier = pltpu.get_barrier_semaphore()

    def greet(device):
        pl.semaphore_signal(barrier, inc=1, device_id=device, device_id_type=MESH)

    ring = Ring(links, place)
    for device in (ring.yp, ring.ym, ring.xp, ring.xm, ring.pair, sib):
        greet(device)
    for dz in (1, -1, 2, -2):
        for flip in (0, 1):
            greet(ring.at_row(ring.rz(dz, flip)))
    end_low, end_high = (r == 0) & (c == 0), (r == 15) & (c == 15)
    pl.when(jnp.logical_not(end_low))(lambda: greet((s, c, z)))
    pl.when(jnp.logical_not(end_high))(lambda: greet((s, c, 8 + z)))
    pl.when(r != c)(lambda: greet((s, c, r)))
    pl.when(c > 0)(lambda: greet((s, r, c - 1)))
    pl.when(r > 0)(lambda: greet((s, r - 1, c)))
    pl.when(c > 0)(lambda: greet((s, r, 0)))

    def one_if(test):
        return test.astype(jnp.int32)

    pl.semaphore_wait(
        barrier,
        16 - one_if(end_low) - one_if(end_high) + one_if(r != c) + one_if(c < 15)
        + one_if(r < 15) + 15 * one_if(c == 0),
    )

    cols_from, cols_sent = transpose_parts(ring, panel.at[0], cols_buf)
    gather_rows(ring, panel.at[0], rows_buf, 16, (5, 4.5, 10, 11, 12, 17, 99))
    gather_cols_ring(ring, cols_from(1), cols_buf.at[1], 8, 5, 100)
    gather_cols_ring(ring, cols_from(0), cols_buf.at[0], 13.2, 5, 190)
    ring.run(until=150)
    loads[3].wait()
    loads[0].wait()
    high, low = halves(rows_buf[...].reshape(512, rows_buf.shape[2]))
    a_high[...] = high
    a_low[...] = low

    def update(part):
        b = halves(cols_buf[part].reshape(256, cols_buf.shape[3]))
        prod = product_nt((a_high[...], a_low[...]), b)
        for w in range(2):
            col = part * 2 + w
            wide[HB + col] = front_v[:, col * BLK : (col + 1) * BLK] - prod[:, w * BLK : (w + 1) * BLK]

    edge = HB * BLK
    half = PBD // 2
    col_pick, row_pick = picks(block_map, s, c), picks(block_map, s, r)
    k_col, k_scatter = links.new(), links.new()
    k_row = [links.new() for _ in range(PBD)]
    k_sib = [links.new(), links.new()]
    spans = ((0, 4), (4, PBD))
    k_scatter_send = [links.new() for _ in range(15)]
    col_to, col_from = (s, r, lax.rem(c + 1, 16)), (s, r, lax.rem(c + 15, 16))
    row_to, row_from = (s, lax.rem(r + 1, 16), c), (s, lax.rem(r + 15, 16), c)

    def col_copy(device):
        return links.copy(k_col, wide.at[pl.ds(CBD, HB)], wide.at[pl.ds(0, HB)], device)

    def row_copies(device, span):
        return [
            links.copy(
                k_row[q], tall.at[q, pl.ds(CBD * BLK, edge)], tall.at[q, pl.ds(0, edge)], device
            )
            for q in range(*span)
        ]

    def spread_cols():
        for q in range(PBD):
            tall[q, edge:, :] = placed_sum(col_pick, q, lambda w: wide[w])

    def send_rows(span):
        @pl.when(r < 15)
        def _():
            for made in row_copies(row_to, span):
                made.start()

    def sib_copy(part):
        first, last = spans[part]
        cols = pl.ds(first, last - first)
        return links.copy(
            k_sib[part], leave.at[pl.ds(half * (1 - s), half), cols],
            come.at[pl.ds(0, half), cols], sib,
        )

    def spread_rows(part):
        @pl.when(r > 0)
        def _():
            for made in row_copies(row_from, spans[part]):
                made.wait_recv()

        for k in range(PBD):
            for q in range(*spans[part]):
                leave[k, q] = placed_sum(
                    row_pick, k, lambda w: tall[q, w * BLK : (w + 1) * BLK, :]
                )
        sib_copy(part).start()

    def assemble(part):
        sib_copy(part).wait_recv()
        for k in range(half):
            for q in range(*spans[part]):
                at = (slice(k * BLK, (k + 1) * BLK), slice(q * BLK, (q + 1) * BLK))
                assembled[at] = parent_v[at] + (leave[half * s + k, q] + come[k, q])

    update(1)
    pl.when((c < 15) & ((c > 0) | (yl == 1)))(lambda: col_copy(col_to).start())
    ring.run()
    update(0)

    @pl.when(r == 0)
    def _():
        tall[:, 0:edge, :] = jnp.zeros((PBD, edge, BLK), F32)

    def scatter(j):
        return links.copy(
            k_scatter_send[j - 1], f_out.at[j], f_rows.at[j], (s, r, jnp.int32(j)), k_scatter
        )

    loads[1].wait()
    loads[2].wait()

    @pl.when(c == 0)
    def _():
        wide[0:HB] = jnp.zeros((HB,) + wide.shape[1:], F32)
        spread_cols()
        send_rows(spans[0])
        pl.when(yl == 0)(lambda: col_copy(col_to).start())
        spread_rows(0)
        assemble(0)
        factor = product_nt(halves(assembled[:, :PANEL]), halves(inverse_v[...]))
        f_out[...] = factor.reshape(f_rows.shape)
        f_rows[0] = f_out[0]
        for j in range(1, 16):
            scatter(j).start()

    def from_col():
        col_copy(col_from).wait_recv()
        spread_cols()
        send_rows(spans[0])

    pl.when(c > 1)(from_col)

    @pl.when(c > 0)
    def _():
        links.copy(k_scatter, f_rows.at[c], f_rows.at[c], (s, r, 0)).wait_recv()

    own = f_rows.at[c]
    cols_here, own_sent = transpose_whole(ring, own, f_cols.at[s])
    gather_rows(ring, own, f_rows, 8, (4, 3.5, 7.5, 7.6, 7.7, 11, 80))
    gather_cols_two(ring, cols_here, f_cols.at[s], f_cols.at[1 - s], (6, 10, 12, 60, 190))
    ring.when(0.1, lambda: pl.when(c == 1)(from_col))
    ring.when(12.5, lambda: send_rows(spans[1]))

    ring.when(50, lambda: pl.when(c > 0)(lambda: spread_rows(0)))
    ring.when(70, lambda: spread_rows(1))
    ring.when(100, lambda: pl.when(c > 0)(lambda: assemble(0)))
    ring.when(100, lambda: assemble(1))
    ring.run()

    f_all = f_rows[...].reshape(assembled.shape[0], PANEL)
    g_all = f_cols[...].reshape(assembled.shape[1], PANEL)
    fh = halves(f_all)
    parent_rows, parent_cols = assembled.shape
    for n in range(3):
        span = slice(n * 256, (n + 1) * 256)
        prod = product_nt(fh, halves(g_all[span]))
        row_at = (r * 2 + s) * parent_rows + lax.broadcasted_iota(jnp.int32, prod.shape, 0)
        col_at_ = c * parent_cols + n * 256 + lax.broadcasted_iota(jnp.int32, prod.shape, 1)
        inside = (row_at >= PANEL) & (col_at_ >= PANEL)
        now = assembled[:, span]
        done = jnp.where(inside, now - prod, now)
        if n < 2:
            done = jnp.where(c == 0, f_all[:, span], done)
        out_v[:, span] = done
    store = pltpu.make_async_copy(out_v, out_ref, local_sems.at[0])
    store.start()

    links.drain()
    cols_sent()
    own_sent()
    pl.when(c < 15)(lambda: col_copy(col_to).wait_send())

    @pl.when(r < 15)
    def _():
        for made in row_copies(row_to, (0, PBD)):
            made.wait_send()

    for part in (0, 1):
        sib_copy(part).wait_send()

    @pl.when(c == 0)
    def _():
        for j in range(1, 16):
            scatter(j).wait_send()

    store.wait()
    assert links.used <= 160, links.used


def shards(front, panel, block_map, parent, inverse):
    anywhere = pl.BlockSpec(memory_space=pl.ANY)
    rows, cols = parent.shape
    kc = panel.shape[2]
    return pl.pallas_call(
        kernel,
        out_shape=jax.ShapeDtypeStruct(parent.shape, F32),
        in_specs=[anywhere, anywhere, pl.BlockSpec(memory_space=pltpu.SMEM), anywhere, anywhere],
        out_specs=anywhere,
        scratch_shapes=[
            pltpu.VMEM((16, 32, kc), F32),
            pltpu.VMEM((2, 16, 16, kc), F32),
            pltpu.VMEM((512, 512), F32),
            pltpu.VMEM((rows, cols), F32),
            pltpu.VMEM((PANEL, PANEL), F32),
            pltpu.VMEM((CBD + HB, 512, BLK), F32),
            pltpu.VMEM((PBD, 768, BLK), F32),
            pltpu.VMEM((PBD, PBD, BLK, BLK), F32),
            pltpu.VMEM((3, PBD, BLK, BLK), F32),
            pltpu.VMEM((rows, cols), F32),
            pltpu.VMEM((16, 24, PANEL), F32),
            pltpu.VMEM((16, 24, PANEL), F32),
            pltpu.VMEM((2, 16, 24, PANEL), F32),
            pltpu.VMEM((rows, cols), F32),
            pltpu.VMEM((512, kc), BF16),
            pltpu.VMEM((512, kc), BF16),
            pltpu.SemaphoreType.DMA((160,)),
            pltpu.SemaphoreType.DMA((160,)),
            pltpu.SemaphoreType.DMA((4,)),
        ],
        compiler_params=pltpu.CompilerParams(
            collective_id=0, has_side_effects=True, vmem_limit_bytes=60 * 2**20
        ),
        name="front_step",
    )(front, panel, block_map, parent, inverse)


def solution(mesh):
    placed = (
        P("sib", "row", "col"), P("sib", ("row", "col"), None), P(),
        P(("row", "sib"), "col"), P(),
    )
    return jax.shard_map(
        shards, mesh=mesh, in_specs=placed, out_specs=P(("row", "sib"), "col"), check_vma=False
    )
```

```python
import functools

import jax
import jax.numpy as jnp
from jax import lax
from jax.experimental import pallas as pl
from jax.experimental.pallas import tpu as pltpu
from jax.sharding import PartitionSpec as P

BLK = 128
CBD = 4
PBD = 6
HB = 2
PANEL = 512
MESH = pl.DeviceIdType.MESH
F32 = jnp.float32
BF16 = jnp.bfloat16


def halves(value):
    high = value.astype(BF16)
    return high, (value - high.astype(F32)).astype(BF16)


def dot_nt(a, b):
    return lax.dot_general(a, b, (((1,), (1,)), ((), ())), preferred_element_type=F32)


def product_nt(a, b):
    a_high, a_low = a
    b_high, b_low = b
    return dot_nt(a_high, b_high) + (dot_nt(a_high, b_low) + dot_nt(a_low, b_high))


class Links:
    def __init__(self, send_sems, recv_sems):
        self.send_sems, self.recv_sems = send_sems, recv_sems
        self.used = 0
        self.sent = []

    def new(self):
        self.used += 1
        return self.used - 1

    def copy(self, k, src, dst, device, k_recv=None):
        return pltpu.make_async_remote_copy(
            src_ref=src,
            dst_ref=dst,
            send_sem=self.send_sems.at[k],
            recv_sem=self.recv_sems.at[k if k_recv is None else k_recv],
            device_id=device,
            device_id_type=MESH,
        )

    def send(self, k, src, dst, device):
        made = self.copy(k, src, dst, device)
        made.start()
        self.sent.append(made)

    def arrived(self, k, ref, device):
        self.copy(k, ref, ref, device).wait_recv()

    def drain(self):
        for made in self.sent:
            made.wait_send()
        self.sent = []


class Ring:
    def __init__(self, links, place):
        self.links = links
        self.s, self.r, self.c = s, r, c = place
        self.z, self.yl = r // 2, lax.rem(r, 2)
        self.x, self.yh = c // 4, lax.rem(c, 4)
        self.yp, self.ym = self.at_col(self.cy(0, 1)), self.at_col(self.cy(0, -1))
        self.xp, self.xm = self.at_col(self.cy(1, 0)), self.at_col(self.cy(-1, 0))
        self.zp, self.zm = self.at_row(self.rz(1)), self.at_row(self.rz(-1))
        self.pair = self.at_row(self.rz(0, 1))
        self.sib = (1 - s, r, c)
        self.events = []

    def cy(self, dx, dy):
        return lax.rem(self.x + dx + 4, 4) * 4 + lax.rem(self.yh + dy + 4, 4)

    def rz(self, dz, flip=0):
        side = 1 - self.yl if flip else self.yl
        return lax.rem(self.z + dz + 8, 8) * 2 + side

    def at_col(self, j):
        return (self.s, self.r, j)

    def at_row(self, i):
        return (self.s, i, self.c)

    def when(self, t, fn):
        self.events.append((t, len(self.events), fn))

    def run(self, until=1e9):
        ready = sorted((e for e in self.events if e[0] < until), key=lambda e: e[:2])
        self.events = [e for e in self.events if e[0] >= until]
        for _, _, fn in ready:
            fn()


def gather_rows(ring, own, rows_buf, cut, times):
    links, c = ring.links, ring.c
    cy, yp, ym, xp, xm = ring.cy, ring.yp, ring.ym, ring.xp, ring.xm
    depth = rows_buf.shape[1]
    top, low = pl.ds(0, cut), pl.ds(cut, depth - cut)
    k_yp, k_ym = links.new(), links.new()
    links.send(k_yp, own, rows_buf.at[c], yp)
    links.send(k_ym, own, rows_buf.at[c], ym)
    k_x = {}
    for dy in (0, -1, 1, 2):
        k_x[dy] = (links.new(), links.new(), links.new(), links.new())

    def spread_x(dy, src=None):
        kp, km, _, _ = k_x[dy]
        slot = cy(0, dy)
        src = rows_buf.at[slot] if src is None else src
        links.send(kp, src, rows_buf.at[slot], xp)
        links.send(km, src, rows_buf.at[slot], xm)

    spread_x(0, own)
    k_y2p, k_y2m = links.new(), links.new()

    def from_ym():
        slot = cy(0, -1)
        links.arrived(k_yp, rows_buf.at[slot], ym)
        links.send(k_y2p, rows_buf.at[slot, top], rows_buf.at[slot, top], yp)
        spread_x(-1)

    def from_yp():
        slot = cy(0, 1)
        links.arrived(k_ym, rows_buf.at[slot], yp)
        links.send(k_y2m, rows_buf.at[slot, low], rows_buf.at[slot, low], ym)
        spread_x(1)

    def far_y():
        slot = cy(0, 2)
        links.arrived(k_y2p, rows_buf.at[slot, top], ym)
        links.arrived(k_y2m, rows_buf.at[slot, low], yp)
        spread_x(2)

    def relay_x(dy):
        kp, km, k2p, k2m = k_x[dy]
        slot_m, slot_p = cy(-1, dy), cy(1, dy)
        links.arrived(kp, rows_buf.at[slot_m], xm)
        links.send(k2p, rows_buf.at[slot_m, top], rows_buf.at[slot_m, top], xp)
        links.arrived(km, rows_buf.at[slot_p], xp)
        links.send(k2m, rows_buf.at[slot_p, low], rows_buf.at[slot_p, low], xm)

    def far_x(dy):
        _, _, k2p, k2m = k_x[dy]
        slot = cy(2, dy)
        links.arrived(k2p, rows_buf.at[slot, top], xm)
        links.arrived(k2m, rows_buf.at[slot, low], xp)

    ring.when(times[0], from_ym)
    ring.when(times[0], from_yp)
    ring.when(times[1], lambda: relay_x(0))
    ring.when(times[2], far_y)
    ring.when(times[3], lambda: relay_x(-1))
    ring.when(times[4], lambda: relay_x(1))
    ring.when(times[5], lambda: relay_x(2))
    ring.when(times[6], lambda: [far_x(dy) for dy in (0, -1, 1, 2)])


def gather_cols_ring(ring, first, cols_buf, t, gap, end):
    links = ring.links
    rz, pair, zp, zm = ring.rz, ring.pair, ring.zp, ring.zm
    depth = cols_buf.shape[1]
    cut = depth // 16 * 8
    parts = (pl.ds(0, cut), pl.ds(cut, depth - cut))
    k_pair = links.new()
    k_z = {(flip, d): (links.new(), links.new()) for flip in (0, 1) for d in (1, 2, 3, 4)}

    def piece(dz, flip, d, way):
        ref = cols_buf.at[rz(dz, flip)]
        return ref.at[parts[way < 0]] if d == 4 else ref

    def step(flip, d):
        for way, k in zip((1, -1), k_z[flip, d]):
            ref = piece(way * (1 - d), flip, d, way)
            links.send(k, ref, ref, zp if way > 0 else zm)

    def relay(flip, d):
        for way, k in zip((1, -1), k_z[flip, d]):
            links.arrived(k, piece(-way * d, flip, d, way), zm if way > 0 else zp)
            if d < 4:
                ref = piece(-way * d, flip, d + 1, way)
                links.send(k_z[flip, d + 1][way < 0], ref, ref, zp if way > 0 else zm)

    def from_first():
        first()
        ref = cols_buf.at[rz(0)]
        links.send(k_pair, ref, ref, pair)
        step(0, 1)

    def from_pair():
        links.arrived(k_pair, cols_buf.at[rz(0, 1)], pair)
        step(1, 1)

    ring.when(t, from_first)
    ring.when(t + gap / 2, from_pair)
    for d in (1, 2, 3, 4):
        ring.when(end if d == 4 else t + gap * d, lambda d=d: relay(0, d))
        ring.when(end if d == 4 else t + gap * (d + 0.5), lambda d=d: relay(1, d))


def gather_cols_two(ring, first, cols_buf, come_buf, times):
    links, yl = ring.links, ring.yl
    rz, pair, sib = ring.rz, ring.pair, ring.sib
    depth = cols_buf.shape[1]
    cut = depth // 16 * 8
    parts = {1: pl.ds(0, cut), -1: pl.ds(cut, depth - cut)}
    k_pair = links.new()
    k_z = {(flip, d): links.new() for flip in (0, 1) for d in (1, -1, 2, -2, 3, -3, 4, -4)}
    k_sib = {(flip, d): links.new() for flip in (0, 1) for d in range(-3, 5)}

    def piece(flip, d):
        ref = cols_buf.at[rz(-d, flip)]
        return ref.at[parts[1 if d > 0 else -1]] if abs(d) == 4 else ref

    def arrived(flip, d):
        links.arrived(k_z[flip, d], piece(flip, d), ring.at_row(rz(-d, flip if abs(d) < 3 else 0)))

    def to_sib(flip, d):
        links.send(k_sib[flip, d], cols_buf.at[rz(d, flip)], cols_buf.at[rz(d, flip)], sib)

    def from_first():
        first()
        ref = cols_buf.at[rz(0)]
        for d in (2, -2, 1, -1):
            for flip in (1, 0):
                links.send(k_z[flip, d], ref, ref, ring.at_row(rz(d, flip)))
        links.send(k_pair, ref, ref, pair)
        to_sib(0, 0)

    def from_near(d):
        for flip in (0, 1):
            arrived(flip, d)
            if abs(d) == 2:
                for e in (3, 4):
                    way = 1 if d > 0 else -1
                    ref = cols_buf.at[rz(-d, flip)]
                    ref = ref.at[parts[way]] if e == 4 else ref
                    links.send(k_z[flip, way * e], ref, ref, ring.at_row(rz(way * (e - 2))))
            to_sib(flip, -d)

    def from_pair():
        links.arrived(k_pair, cols_buf.at[rz(0, 1)], pair)
        to_sib(1, 0)

    def from_far():
        for flip in (0, 1):
            for d in (3, -3):
                arrived(flip, d)
                to_sib(flip, -d)
        for flip in (0, 1):
            arrived(flip, 4)
            arrived(flip, -4)
            to_sib(flip, 4)

    def from_sib():
        for (flip, d), k in k_sib.items():
            links.arrived(k, come_buf.at[rz(d, flip)], sib)

    ring.when(times[0], from_first)
    for d in (2, -2):
        ring.when(times[1], lambda d=d: from_near(d))
    ring.when(times[2], from_pair)
    for d in (1, -1):
        ring.when(times[2], lambda d=d: from_near(d))
    ring.when(times[3], from_far)
    ring.when(times[4], from_sib)


def transpose_whole(ring, own, cols_buf):
    links, s, r, c = ring.links, ring.s, ring.r, ring.c
    k = links.new()
    there = (s, c, r)

    @pl.when(r != c)
    def _():
        links.copy(k, own, cols_buf.at[c], there).start()

    @pl.when(r == c)
    def _():
        pltpu.make_async_copy(own, cols_buf.at[r], links.recv_sems.at[k]).start()

    def sent():
        @pl.when(r != c)
        def _():
            links.copy(k, own, cols_buf.at[c], there).wait_send()

    return (lambda: links.arrived(k, cols_buf.at[r], there)), sent


def transpose_parts(ring, own, cols_buf):
    links, s, r, c = ring.links, ring.s, ring.r, ring.c
    k = [links.new(), links.new()]
    k_send = [links.new(), links.new()]
    part, at = c // 8, lax.rem(c, 8)
    rows = [pl.ds(0, 16), pl.ds(16, 16)]

    def here(h):
        return (r == c) & (at * 2 + h == r)

    def copy(h, p):
        return links.copy(k_send[h], own.at[rows[h]], cols_buf.at[p, at * 2 + h], (s, at * 2 + h, r), k[p])

    for h in (0, 1):
        for p in (0, 1):

            @pl.when(jnp.logical_not(here(h)) & (part == p))
            def _():
                copy(h, p).start()

            @pl.when(here(h) & (part == p))
            def _():
                pltpu.make_async_copy(own.at[rows[h]], cols_buf.at[p, r], links.recv_sems.at[k[p]]).start()

    def sent():
        for h in (0, 1):

            @pl.when(jnp.logical_not(here(h)))
            def _():
                copy(h, 0).wait_send()

    def arrived(p):
        return lambda: links.arrived(k[p], cols_buf.at[p, r], (s, c, p * 8 + ring.z))

    return arrived, sent


def picks(block_map, child, group):
    weights = {}
    for w in range(CBD + HB):
        i = lax.rem(group * CBD - HB + w + 64, 64)
        mark = block_map[child, i] - group * PBD
        for q in range(max(0, w - HB), min(PBD, w + HB + 1)):
            weights[w, q] = (mark == q).astype(F32)
    return weights


def placed_sum(weights, q, block):
    total = None
    for w in range(CBD + HB):
        if (w, q) in weights:
            term = weights[w, q] * block(w)
            total = term if total is None else total + term
    return total


def kernel(
    front, panel, block_map, parent, inverse, out_ref,
    rows_buf, cols_buf, front_v, parent_v, inverse_v,
    wide, tall, edge_in, leave, come, assembled, f_out, f_rows, f_cols, out_v,
    a_high, a_low, send_sems, recv_sems, local_sems,
):
    s, r, c = lax.axis_index("sib"), lax.axis_index("row"), lax.axis_index("col")
    place = (s, r, c)
    z, yl = r // 2, lax.rem(r, 2)
    x, yh = c // 4, lax.rem(c, 4)
    links = Links(send_sems, recv_sems)
    sib = (1 - s, r, c)

    loads = [
        pltpu.make_async_copy(src, dst, local_sems.at[k])
        for k, (src, dst) in enumerate(
            ((front.at[0], front_v), (parent, parent_v), (inverse, inverse_v),
             (panel.at[0], rows_buf.at[c]))
        )
    ]
    for load in loads:
        load.start()

    barrier = pltpu.get_barrier_semaphore()

    def greet(device):
        pl.semaphore_signal(barrier, inc=1, device_id=device, device_id_type=MESH)

    ring = Ring(links, place)
    for device in (ring.yp, ring.ym, ring.xp, ring.xm, ring.pair, sib):
        greet(device)
    for dz in (1, -1, 2, -2):
        for flip in (0, 1):
            greet(ring.at_row(ring.rz(dz, flip)))
    end_low, end_high = (r == 0) & (c == 0), (r == 15) & (c == 15)
    pl.when(jnp.logical_not(end_low))(lambda: greet((s, c, z)))
    pl.when(jnp.logical_not(end_high))(lambda: greet((s, c, 8 + z)))
    pl.when(r != c)(lambda: greet((s, c, r)))
    pl.when(c > 0)(lambda: greet((s, r, c - 1)))
    pl.when(r > 0)(lambda: greet((s, r - 1, c)))
    pl.when(c > 0)(lambda: greet((s, r, 0)))

    def one_if(test):
        return test.astype(jnp.int32)

    pl.semaphore_wait(
        barrier,
        16 - one_if(end_low) - one_if(end_high) + one_if(r != c) + one_if(c < 15)
        + one_if(r < 15) + 15 * one_if(c == 0),
    )

    cols_from, cols_sent = transpose_parts(ring, panel.at[0], cols_buf)
    gather_cols_ring(ring, cols_from(1), cols_buf.at[1], 8, 5, 100)
    gather_cols_ring(ring, cols_from(0), cols_buf.at[0], 13.2, 5, 190)
    ring.run(until=13.3)
    gather_rows(ring, panel.at[0], rows_buf, 16, (19, 18.5, 24, 25, 26, 31, 99))
    ring.run(until=150)
    loads[3].wait()
    loads[0].wait()
    high, low = halves(rows_buf[...].reshape(512, rows_buf.shape[2]))
    a_high[...] = high
    a_low[...] = low

    def update(part):
        b = halves(cols_buf[part].reshape(256, cols_buf.shape[3]))
        prod = product_nt((a_high[...], a_low[...]), b)
        for w in range(2):
            col = part * 2 + w
            wide[HB + col] = front_v[:, col * BLK : (col + 1) * BLK] - prod[:, w * BLK : (w + 1) * BLK]

    edge = HB * BLK
    half = PBD // 2
    col_pick, row_pick = picks(block_map, s, c), picks(block_map, s, r)
    k_col, k_scatter = links.new(), links.new()
    k_row = [links.new() for _ in range(PBD)]
    k_edge = [links.new(), links.new()]
    k_sib = [links.new(), links.new()]
    spans = ((0, 4), (4, PBD))
    k_scatter_send = [links.new() for _ in range(15)]
    col_to, col_from = (s, r, lax.rem(c + 1, 16)), (s, r, lax.rem(c + 15, 16))
    row_to, row_from = (s, lax.rem(r + 1, 16), c), (s, lax.rem(r + 15, 16), c)

    def col_copy(device):
        return links.copy(k_col, wide.at[pl.ds(CBD, HB)], wide.at[pl.ds(0, HB)], device)

    def row_copies(device, span):
        return [
            links.copy(
                k_row[q], tall.at[q, pl.ds(CBD * BLK, edge)], tall.at[q, pl.ds(0, edge)], device
            )
            for q in range(*span)
        ]

    def spread_cols():
        for q in range(PBD):
            tall[q, edge:, :] = placed_sum(col_pick, q, lambda w: wide[w])

    def edge_copy(part, device):
        return links.copy(
            k_edge[part], wide.at[pl.ds(HB + 2 * part, 2), pl.ds(edge, edge)],
            edge_in.at[pl.ds(2 * part, 2)], device,
        )

    def send_edge(part):
        pl.when((c == 0) & (r < 15))(lambda: edge_copy(part, row_to).start())

    def spread_edge():
        @pl.when(r > 0)
        def _():
            for part in (1, 0):
                edge_copy(part, row_from).wait_recv()
            own_pick = {k: v for k, v in col_pick.items() if k[0] >= HB}
            for q in range(PBD):
                tall[q, 0:edge, :] = placed_sum(own_pick, q, lambda w: edge_in[w - HB])

    def send_rows(span):
        @pl.when((r < 15) & (c > 0))
        def _():
            for made in row_copies(row_to, span):
                made.start()

    def sib_copy(part):
        first, last = spans[part]
        cols = pl.ds(first, last - first)
        return links.copy(
            k_sib[part], leave.at[pl.ds(half * (1 - s), half), cols],
            come.at[pl.ds(0, half), cols], sib,
        )

    def spread_rows(part):
        @pl.when((r > 0) & (c > 0))
        def _():
            for made in row_copies(row_from, spans[part]):
                made.wait_recv()

        for k in range(PBD):
            for q in range(*spans[part]):
                leave[k, q] = placed_sum(
                    row_pick, k, lambda w: tall[q, w * BLK : (w + 1) * BLK, :]
                )
        sib_copy(part).start()

    def assemble(part):
        sib_copy(part).wait_recv()
        for k in range(half):
            for q in range(*spans[part]):
                at = (slice(k * BLK, (k + 1) * BLK), slice(q * BLK, (q + 1) * BLK))
                assembled[at] = parent_v[at] + (leave[half * s + k, q] + come[k, q])

    update(1)
    send_edge(1)
    pl.when((c < 15) & ((c > 0) | (yl == 1)))(lambda: col_copy(col_to).start())
    ring.run()
    update(0)
    send_edge(0)

    @pl.when(r == 0)
    def _():
        tall[:, 0:edge, :] = jnp.zeros((PBD, edge, BLK), F32)

    def scatter(j):
        return links.copy(
            k_scatter_send[j - 1], f_out.at[j], f_rows.at[j], (s, r, jnp.int32(j)), k_scatter
        )

    loads[1].wait()
    loads[2].wait()

    @pl.when(c == 0)
    def _():
        wide[0:HB] = jnp.zeros((HB,) + wide.shape[1:], F32)
        spread_cols()
        pl.when(yl == 0)(lambda: col_copy(col_to).start())
        spread_edge()
        spread_rows(0)
        assemble(0)
        factor = product_nt(halves(assembled[:, :PANEL]), halves(inverse_v[...]))
        f_out[...] = factor.reshape(f_rows.shape)
        f_rows[0] = f_out[0]
        for j in range(1, 16):
            scatter(j).start()

    def from_col():
        col_copy(col_from).wait_recv()
        spread_cols()
        send_rows(spans[0])

    pl.when(c > 1)(from_col)

    @pl.when(c > 0)
    def _():
        links.copy(k_scatter, f_rows.at[c], f_rows.at[c], (s, r, 0)).wait_recv()

    own = f_rows.at[c]
    cols_here, own_sent = transpose_whole(ring, own, f_cols.at[s])
    gather_rows(ring, own, f_rows, 8, (4, 3.5, 7.5, 7.6, 7.7, 11, 80))
    gather_cols_two(ring, cols_here, f_cols.at[s], f_cols.at[1 - s], (6, 10, 12, 60, 190))
    ring.when(0.1, lambda: pl.when(c == 1)(from_col))
    ring.when(12.5, lambda: send_rows(spans[1]))

    ring.when(50, lambda: pl.when(c > 0)(lambda: spread_rows(0)))
    ring.when(70, lambda: spread_rows(1))
    ring.when(100, lambda: pl.when(c > 0)(lambda: assemble(0)))
    ring.when(100, lambda: assemble(1))
    ring.run()

    f_all = f_rows[...].reshape(assembled.shape[0], PANEL)
    g_all = f_cols[...].reshape(assembled.shape[1], PANEL)
    fh = halves(f_all)
    parent_rows, parent_cols = assembled.shape
    for n in range(3):
        span = slice(n * 256, (n + 1) * 256)
        prod = product_nt(fh, halves(g_all[span]))
        row_at = (r * 2 + s) * parent_rows + lax.broadcasted_iota(jnp.int32, prod.shape, 0)
        col_at_ = c * parent_cols + n * 256 + lax.broadcasted_iota(jnp.int32, prod.shape, 1)
        inside = (row_at >= PANEL) & (col_at_ >= PANEL)
        now = assembled[:, span]
        done = jnp.where(inside, now - prod, now)
        if n < 2:
            done = jnp.where(c == 0, f_all[:, span], done)
        out_v[:, span] = done
    store = pltpu.make_async_copy(out_v, out_ref, local_sems.at[0])
    store.start()

    links.drain()
    cols_sent()
    own_sent()
    pl.when(c < 15)(lambda: col_copy(col_to).wait_send())

    @pl.when((r < 15) & (c > 0))
    def _():
        for made in row_copies(row_to, (0, PBD)):
            made.wait_send()

    @pl.when((r < 15) & (c == 0))
    def _():
        for part in (0, 1):
            edge_copy(part, row_to).wait_send()

    for part in (0, 1):
        sib_copy(part).wait_send()

    @pl.when(c == 0)
    def _():
        for j in range(1, 16):
            scatter(j).wait_send()

    store.wait()
    assert links.used <= 160, links.used


def shards(front, panel, block_map, parent, inverse):
    anywhere = pl.BlockSpec(memory_space=pl.ANY)
    rows, cols = parent.shape
    kc = panel.shape[2]
    return pl.pallas_call(
        kernel,
        out_shape=jax.ShapeDtypeStruct(parent.shape, F32),
        in_specs=[anywhere, anywhere, pl.BlockSpec(memory_space=pltpu.SMEM), anywhere, anywhere],
        out_specs=anywhere,
        scratch_shapes=[
            pltpu.VMEM((16, 32, kc), F32),
            pltpu.VMEM((2, 16, 16, kc), F32),
            pltpu.VMEM((512, 512), F32),
            pltpu.VMEM((rows, cols), F32),
            pltpu.VMEM((PANEL, PANEL), F32),
            pltpu.VMEM((CBD + HB, 512, BLK), F32),
            pltpu.VMEM((PBD, 768, BLK), F32),
            pltpu.VMEM((CBD, 256, BLK), F32),
            pltpu.VMEM((PBD, PBD, BLK, BLK), F32),
            pltpu.VMEM((3, PBD, BLK, BLK), F32),
            pltpu.VMEM((rows, cols), F32),
            pltpu.VMEM((16, 24, PANEL), F32),
            pltpu.VMEM((16, 24, PANEL), F32),
            pltpu.VMEM((2, 16, 24, PANEL), F32),
            pltpu.VMEM((rows, cols), F32),
            pltpu.VMEM((512, kc), BF16),
            pltpu.VMEM((512, kc), BF16),
            pltpu.SemaphoreType.DMA((160,)),
            pltpu.SemaphoreType.DMA((160,)),
            pltpu.SemaphoreType.DMA((4,)),
        ],
        compiler_params=pltpu.CompilerParams(
            collective_id=0, has_side_effects=True, vmem_limit_bytes=60 * 2**20
        ),
        name="front_step",
    )(front, panel, block_map, parent, inverse)


def solution(mesh):
    placed = (
        P("sib", "row", "col"), P("sib", ("row", "col"), None), P(),
        P(("row", "sib"), "col"), P(),
    )
    return jax.shard_map(
        shards, mesh=mesh, in_specs=placed, out_specs=P(("row", "sib"), "col"), check_vma=False
    )
```
